256 devices in a mesh: row: 4 (over y), col: 64 (over z, x, core).
Axes of the slice: x: 4, y: 4, z: 8, core: 2. Of those that a mesh axis runs over, the one named last changes fastest.
Arguments:
- momentum: bfloat16 [12288, 26624], P('row', 'col'), may hold values from -120 to 120
- gradient: bfloat16 [12288, 26624], P('row', 'col'), may hold values from -120 to 120
- right_basis: float32 [26624, 512], P('col'), may hold values from -0.0390625 to 0.0390625
Outputs:
- new_momentum: bfloat16 [12288, 26624], P('row', 'col')
- new_basis: float32 [26624, 512], P('col')
- direction: bfloat16 [12288, 26624], P('row', 'col')
The draws below stay inside these ranges and needn't reach their ends.
All inputs are finite; a program needn't handle non-finite values.
Results may differ from the reference program's by a relative error of at most 0.024.
Values may be sent and summed in bfloat16 or wider, within the bound.
No kernel may reach another device: no remote copies, remote signals or barrier semaphores. Data moves between devices by JAX's collectives and lax.ppermute only.
A program may use at most 128 MiB of HBM per device.

```python
import math
import jax
import jax.numpy as jnp
from jax import lax

D = 12288
FF = 26624
RANK = 512


def draw_momentum(key, part):
    key = jax.random.fold_in(key, 11)
    first, second, third = jax.random.split(key, 3)
    col_trend = 3.0 ** (jnp.arange(FF, dtype=jnp.float32) / (FF - 1))
    col_scale = jnp.exp(jax.random.uniform(second, (FF,), minval=0.0, maxval=math.log(10.0))) * col_trend
    values = jnp.clip(jax.random.normal(first, (D, FF)), -4.0, 4.0)
    row_scale = jnp.exp(jax.random.uniform(third, (D,), minval=0.0, maxval=math.log(10.0)))
    return (0.1 * values * row_scale[:, None] * col_scale[None, :]).astype(jnp.bfloat16)


def draw_gradient(key, part):
    key = jax.random.fold_in(key, 23)
    first, second, third = jax.random.split(key, 3)
    col_trend = 3.0 ** (jnp.arange(FF, dtype=jnp.float32) / (FF - 1))
    col_scale = jnp.exp(jax.random.uniform(second, (FF,), minval=0.0, maxval=math.log(10.0))) * col_trend
    values = jnp.clip(jax.random.normal(first, (D, FF)), -4.0, 4.0)
    row_scale = jnp.exp(jax.random.uniform(third, (D,), minval=0.0, maxval=math.log(10.0)))
    return (0.1 * values * row_scale[:, None] * col_scale[None, :]).astype(jnp.bfloat16)


def steps_of(stream_key, shape, cuts, low, largest):
    factor_of, own = 1.0, jax.random.fold_in(stream_key, 6)
    for dim, shards_of in cuts:
        draws = jnp.exp(jax.random.uniform(jax.random.fold_in(own, dim), (shards_of,), jnp.float32, low / len(cuts), largest / len(cuts)))
        factor_of = factor_of * jnp.repeat(draws, shape[dim] // shards_of).reshape([-1 if axis == dim else 1 for axis in range(len(shape))])
    return factor_of


def bell_draw(own_key, shape, scale, most, pieces=(), kind=jnp.bfloat16):
    loudness = steps_of(own_key, shape, pieces, -0.22, 0.18) if pieces else 1.0
    array = jax.random.normal(own_key, shape, jnp.float32) * scale * loudness
    return jnp.minimum(jnp.maximum(array, -most), most).astype(kind)


def setup_inputs(seed: int = 0) -> dict:
    splits = jax.random.split(jax.random.key(seed), 4)
    return {
        "momentum": draw_momentum(jax.random.fold_in(splits[3], 71), 0),
        "gradient": draw_gradient(jax.random.fold_in(splits[3], 71), 0),
        "right_basis": bell_draw(splits[2], (FF, RANK), FF ** -0.5, 0.0390625, ((0, 64),), jnp.float32),
    }


error_share = 0.05
epsilon = 1e-06

def reference(momentum, gradient, right_basis):
    blended = (momentum.astype(jnp.float32) + gradient.astype(jnp.float32)).astype(jnp.bfloat16)
    basis_half = right_basis.astype(jnp.bfloat16)
    projected = jnp.dot(blended.astype(jnp.float32), basis_half.astype(jnp.float32), preferred_element_type=jnp.float32)
    gram_matrix = jnp.dot(projected.T.astype(jnp.float32), projected.astype(jnp.float32), precision=lax.Precision.HIGHEST, preferred_element_type=jnp.float32)
    chol_factor = jnp.linalg.cholesky(gram_matrix)
    orthonormal = lax.linalg.triangular_solve(chol_factor, projected, left_side=False, lower=True, transpose_a=True)
    ortho_half = orthonormal.astype(jnp.bfloat16)
    back_proj = jnp.dot(blended.T.astype(jnp.float32), ortho_half.astype(jnp.float32), preferred_element_type=jnp.float32)
    back_half = back_proj.astype(jnp.bfloat16)
    low_rank = jnp.dot(ortho_half.astype(jnp.float32), back_half.T.astype(jnp.float32), preferred_element_type=jnp.float32)
    new_momentum = (blended.astype(jnp.float32) - error_share * low_rank).astype(jnp.bfloat16)
    col_sq = lax.optimization_barrier(jnp.sum(back_proj * back_proj, axis=0))
    new_basis = back_proj / (jnp.sqrt(col_sq) + epsilon)
    scale_factor = math.sqrt(D * FF / RANK)
    direction = (jnp.dot(ortho_half.astype(jnp.float32), new_basis.astype(jnp.bfloat16).T.astype(jnp.float32), preferred_element_type=jnp.float32) * scale_factor).astype(jnp.bfloat16)
    return (new_momentum, new_basis, direction)
```

```python
import math

import jax
import jax.numpy as jnp
from jax import lax
from jax.experimental import pallas as pl
from jax.experimental.pallas import tpu as pltpu
from jax.sharding import Mesh
from jax.sharding import PartitionSpec as P

RANK = 512
NB = 128
HI = lax.Precision.HIGHEST
F32 = jnp.float32
BF16 = jnp.bfloat16
error_share = 0.05
epsilon = 1e-06


def factor_block(d_ref, x_ref, sub):
    groups = NB // 8
    wide = (8, NB)
    for b in range(groups):
        r0 = 8 * b
        rows_d = d_ref[r0 : r0 + 8, :]
        rows_x = x_ref[r0 : r0 + 8, :]
        cols = [jnp.broadcast_to(rows_d[:, r0 + j : r0 + j + 1], wide) for j in range(8)]
        pivots = jnp.ones(wide, F32)
        row_d, row_x, inverse, coef = [], [], [], {}
        for k in range(8):
            pivot = jnp.broadcast_to(cols[k][k : k + 1, :], wide)
            recip = 1.0 / pivot
            pivots = jnp.where(sub == k, pivot, pivots)
            dk = jnp.broadcast_to(rows_d[k : k + 1, :], wide)
            xk = jnp.broadcast_to(rows_x[k : k + 1, :], wide)
            factor = jnp.where(sub > k, cols[k] * recip, 0.0)
            for j in range(k + 1, 8):
                coef[k, j] = jnp.broadcast_to(cols[j][k : k + 1, :], wide)
                cols[j] = cols[j] - factor * coef[k, j]
            rows_d = rows_d - factor * dk
            rows_x = rows_x - factor * xk
            row_d.append(dk)
            row_x.append(xk)
            inverse.append(recip)
        x_ref[r0 : r0 + 8, :] = rows_x * lax.rsqrt(pivots)
        for v in range(b + 1, groups):
            q = 8 * v
            low_d = d_ref[q : q + 8, :]
            low_x = x_ref[q : q + 8, :]
            lead = [jnp.broadcast_to(low_d[:, r0 + j : r0 + j + 1], wide) for j in range(8)]
            for k in range(8):
                factor = lead[k] * inverse[k]
                for j in range(k + 1, 8):
                    lead[j] = lead[j] - factor * coef[k, j]
                low_d = low_d - factor * row_d[k]
                low_x = low_x - factor * row_x[k]
            d_ref[q : q + 8, :] = low_d
            x_ref[q : q + 8, :] = low_x


def eye(size):
    row = lax.broadcasted_iota(jnp.int32, (size, size), 0)
    col = lax.broadcasted_iota(jnp.int32, (size, size), 1)
    return jnp.where(row == col, 1.0, 0.0).astype(F32)


def chol_kernel(g_ref, o_ref, a_ref, d_ref, x_ref):
    sub = lax.broadcasted_iota(jnp.int32, (8, NB), 0)
    a_ref[...] = g_ref[...]
    o_ref[...] = eye(RANK)
    lane = lax.broadcasted_iota(jnp.int32, (NB, RANK), 1)

    def step(p, carry):
        at = pl.multiple_of(p * NB, NB)
        rows = pl.ds(at, NB)
        d_ref[...] = a_ref[rows, rows]
        x_ref[...] = eye(NB)
        factor_block(d_ref, x_ref, sub)
        block = x_ref[...]
        upper = jnp.dot(block, a_ref[rows, :], precision=HI, preferred_element_type=F32)
        done = jnp.dot(block, o_ref[rows, :], precision=HI, preferred_element_type=F32)
        o_ref[rows, :] = done
        below = jnp.where(lane >= at + NB, upper, 0.0)
        dims = (((0,), (0,)), ((), ()))
        a_ref[...] -= lax.dot_general(below, upper, dims, precision=HI, preferred_element_type=F32)
        o_ref[...] -= lax.dot_general(below, done, dims, precision=HI, preferred_element_type=F32)
        return carry

    lax.fori_loop(0, RANK // NB, step, 0)


def inverse_factor(gram):
    return pl.pallas_call(
        chol_kernel,
        out_shape=jax.ShapeDtypeStruct((RANK, RANK), F32),
        scratch_shapes=[
            pltpu.VMEM((RANK, RANK), F32),
            pltpu.VMEM((NB, NB), F32),
            pltpu.VMEM((NB, NB), F32),
        ],
        compiler_params=pltpu.CompilerParams(vmem_limit_bytes=24 * 1024 * 1024),
        cost_estimate=pl.CostEstimate(flops=20_000_000_000, bytes_accessed=2 * RANK * RANK * 4, transcendentals=0),
        name="inverse_factor",
    )(gram)


def swap(block, axis):
    return lax.all_to_all(block, axis, 0, 0, tiled=True)


def scatter_sum(block, axis, n):
    rows = block.shape[0] // n
    got = swap(block.reshape(n, rows, RANK), axis)
    return jnp.sum(got.astype(F32), axis=0).astype(BF16)


def gather(block, axis, n):
    got = swap(jnp.broadcast_to(block[None], (n, *block.shape)), axis)
    return got.reshape(n * block.shape[0], RANK)


def shift(value, axis, n, by):
    return lax.ppermute(value, axis, [(i, (i + by) % n) for i in range(n)])


def row_sum(block, n):
    me = lax.axis_index("row")
    rows = block.shape[0] // n
    pieces = block.reshape(n, rows, RANK)
    piece = lambda i: lax.dynamic_index_in_dim(pieces, lax.rem(i, n), 0, keepdims=False)
    total = piece(me).astype(F32)
    for by in range(1, n):
        total = total + shift(piece(me + by), "row", n, by).astype(F32)
    mine = total.astype(BF16)
    held = jnp.stack([mine] + [shift(mine, "row", n, by) for by in range(1, n)])
    return jnp.concatenate(
        [lax.dynamic_index_in_dim(held, lax.rem(me - i + n, n), 0, keepdims=False) for i in range(n)]
    )


def butterfly(value, sizes):
    for axis, n in sizes:
        step = 1
        while step < n:
            value = value + lax.ppermute(value, axis, [(i, i ^ step) for i in range(n)])
            step *= 2
    return value


def shards(sizes, whole, momentum, gradient, right_basis):
    core = lax.axis_index("core")
    blended = (momentum.astype(F32) + gradient.astype(F32)).astype(BF16)
    basis_half = right_basis.astype(BF16)
    part = jnp.dot(blended, basis_half, preferred_element_type=F32).astype(BF16)
    for axis in ("core", "x", "z"):
        part = scatter_sum(part, axis, sizes[axis])
    for axis in ("z", "x"):
        part = gather(part, axis, sizes[axis])
    other = shift(part, "core", 2, 1)
    gram_part = lax.dot_general(part, part, (((0,), (0,)), ((), ())), preferred_element_type=F32).astype(BF16)
    both = ("row", "core")
    gram = gather(scatter_sum(gram_part, both, sizes["row"] * 2), both, sizes["row"] * 2).astype(F32)
    first = core == 0
    projected = jnp.concatenate([jnp.where(first, part, other), jnp.where(first, other, part)])
    cross = lax.dot_general(blended, projected, (((0,), (0,)), ((), ())), preferred_element_type=F32)
    cross = row_sum(cross.astype(BF16), sizes["row"])
    inverse = inverse_factor(gram).astype(BF16)
    times = (((1,), (1,)), ((), ()))
    back_proj = lax.dot_general(cross, inverse, times, preferred_element_type=F32)
    col_sq = jnp.sum(back_proj * back_proj, axis=0, keepdims=True)
    col_sq = butterfly(col_sq, [(axis, sizes[axis]) for axis in ("core", "x", "z")])
    ortho_half = lax.dot_general(projected, inverse, times, preferred_element_type=F32).astype(BF16)
    back_half = back_proj.astype(BF16)
    low_rank = lax.dot_general(ortho_half, back_half, times, preferred_element_type=F32)
    new_momentum = (blended.astype(F32) - error_share * low_rank).astype(BF16)
    new_basis = back_proj / (jnp.sqrt(col_sq) + epsilon)
    product = lax.dot_general(ortho_half, new_basis.astype(BF16), times, preferred_element_type=F32)
    direction = (product * math.sqrt(whole / RANK)).astype(BF16)
    return (new_momentum, new_basis, direction)


def solution(mesh):
    sizes = {"row": 4, "z": 8, "x": 4, "core": 2}
    inner = Mesh(mesh.devices.reshape(tuple(sizes.values())), tuple(sizes))
    col = ("z", "x", "core")

    def step(momentum, gradient, right_basis):
        whole = momentum.shape[0] * momentum.shape[1]
        body = lambda *args: shards(sizes, whole, *args)
        return jax.shard_map(
            body,
            mesh=inner,
            in_specs=(P("row", col), P("row", col), P(col, None)),
            out_specs=(P("row", col), P(col, None), P("row", col)),
            check_vma=False,
        )(momentum, gradient, right_basis)

    return step
```

```python
import math

import jax
import jax.numpy as jnp
from jax import lax
from jax.experimental import pallas as pl
from jax.experimental.pallas import tpu as pltpu
from jax.sharding import Mesh
from jax.sharding import PartitionSpec as P

RANK = 512
NB = 128
F32 = jnp.float32
BF16 = jnp.bfloat16
error_share = 0.05
epsilon = 1e-06


def split(value):
    high = value.astype(BF16)
    return high, (value - high.astype(F32)).astype(BF16)


def product3(left, right, dims):
    left_high, left_low = split(left)
    right_high, right_low = split(right)
    dot = lambda a, b: lax.dot_general(a, b, dims, preferred_element_type=F32)
    return dot(left_high, right_high) + (dot(left_high, right_low) + dot(left_low, right_high))


def factor_block(w_ref, sub, lane):
    groups = NB // 8
    wide = (8, NB)
    row_of = lambda value, k: jnp.broadcast_to(value[k : k + 1, :], wide)
    columns = lambda value, at: [jnp.broadcast_to(value[:, at + j : at + j + 1], wide) for j in range(8)]
    for b in range(groups):
        r0 = 8 * b
        mine = (lane >= r0) & (lane < r0 + 8)
        more = b + 1 < groups
        top = w_ref[r0 : r0 + 8, :]
        cols = columns(top, r0)
        top = jnp.where(mine, jnp.where(lane - r0 == sub, 1.0, 0.0), top)
        if more:
            below = w_ref[r0 + 8 : r0 + 16, :]
            next_cols = columns(below, r0)
            below = jnp.where(mine, 0.0, below)
        pivots = jnp.ones(wide, F32)
        rows, inverse, coef = [], [], {}
        for k in range(8):
            pivot = row_of(cols[k], k)
            recip = 1.0 / pivot
            pivots = jnp.where(sub == k, pivot, pivots)
            row = row_of(top, k)
            factor = jnp.where(sub > k, cols[k] * recip, 0.0)
            if more:
                next_factor = next_cols[k] * recip
            for j in range(k + 1, 8):
                coef[k, j] = row_of(cols[j], k)
                cols[j] = cols[j] - factor * coef[k, j]
                if more:
                    next_cols[j] = next_cols[j] - next_factor * coef[k, j]
            top = top - factor * row
            if more:
                below = below - next_factor * row
            rows.append(row)
            inverse.append(recip)
        w_ref[r0 : r0 + 8, :] = top * lax.rsqrt(pivots)
        if more:
            w_ref[r0 + 8 : r0 + 16, :] = below
        for v in range(b + 2, groups):
            q = 8 * v
            low = w_ref[q : q + 8, :]
            lead = columns(low, r0)
            low = jnp.where(mine, 0.0, low)
            for k in range(8):
                factor = lead[k] * inverse[k]
                for j in range(k + 1, 8):
                    lead[j] = lead[j] - factor * coef[k, j]
                low = low - factor * rows[k]
            w_ref[q : q + 8, :] = low


def chol_kernel(pos_ref, mine_ref, other_ref, half_ref, o_ref, w_ref):
    sub = lax.broadcasted_iota(jnp.int32, (8, NB), 0)
    lane = lax.broadcasted_iota(jnp.int32, (8, NB), 1)
    lower = lax.broadcasted_iota(jnp.int32, (NB, NB), 0) >= lax.broadcasted_iota(jnp.int32, (NB, NB), 1)
    wide_lane = lax.broadcasted_iota(jnp.int32, (NB, RANK), 1)
    tall_row = lax.broadcasted_iota(jnp.int32, (RANK, NB), 0)
    pieces = 4
    tall = mine_ref.shape[0] // pieces
    for j in range(pieces):
        at = ((pos_ref[2] - j) & (pieces - 1)) * tall
        here = slice(j * tall, (j + 1) * tall)
        o_ref[pl.ds(pl.multiple_of(at + pos_ref[0] * (RANK // 2), tall), tall), :] = mine_ref[here, :].astype(F32)
        o_ref[pl.ds(pl.multiple_of(at + (1 - pos_ref[0]) * (RANK // 2), tall), tall), :] = other_ref[here, :].astype(F32)

    def step(p, carry):
        at = pl.multiple_of(p * NB, NB)
        here = pl.ds(at, NB)
        w_ref[...] = o_ref[here, here]
        factor_block(w_ref, sub, lane)
        block = jnp.where(lower, w_ref[...], 0.0)
        panel = product3(block, o_ref[here, :], (((1,), (0,)), ((), ())))
        o_ref[here, :] = panel
        o_ref[here, here] = block
        rest = jnp.where(wide_lane >= at + NB, panel, 0.0)
        o_ref[:, here] = jnp.where(tall_row >= at + NB, 0.0, o_ref[:, here])
        o_ref[...] -= product3(rest, o_ref[here, :], (((0,), (0,)), ((), ())))
        return carry

    lax.fori_loop(0, RANK // NB, step, 0)
    row = lax.broadcasted_iota(jnp.int32, (RANK, RANK), 0)
    col = lax.broadcasted_iota(jnp.int32, (RANK, RANK), 1)
    half_ref[...] = jnp.where(row >= col, o_ref[...], 0.0).astype(BF16)


SMEM = pl.BlockSpec(memory_space=pltpu.SMEM)
VMEM = pl.BlockSpec(memory_space=pltpu.VMEM)


def local(kernel, name, ins, outs, flops, scratch=()):
    shapes = [jax.ShapeDtypeStruct(shape, dtype) for shape, dtype in outs]
    moved = sum(v.size * v.dtype.itemsize for v in (*ins, *shapes))
    return pl.pallas_call(
        kernel,
        out_shape=shapes,
        in_specs=[SMEM] + [VMEM] * (len(ins) - 1),
        out_specs=[VMEM] * len(outs),
        scratch_shapes=[pltpu.VMEM(shape, dtype) for shape, dtype in scratch],
        compiler_params=pltpu.CompilerParams(vmem_limit_bytes=6 * 1024 * 1024),
        cost_estimate=pl.CostEstimate(flops=flops, bytes_accessed=moved, transcendentals=0),
        name=name,
    )(*ins)


def inverse_factor(pos, mine, other):
    square = (RANK, RANK)
    return local(
        chol_kernel,
        "inverse_factor",
        (pos, mine, other),
        [(square, BF16)],
        20_000_000_000,
        [(square, F32), ((NB, NB), F32)],
    )[0]


def swap(pieces, axis):
    return lax.all_to_all(pieces, axis, 0, 0, tiled=True)


def scatter_swap(block, axis, n):
    got = swap(block.reshape(n, block.shape[0] // n, RANK), axis)
    return jnp.sum(got.astype(F32), axis=0).astype(BF16)


def gather_swap(block, axis, n):
    got = swap(jnp.broadcast_to(block[None], (n, *block.shape)), axis)
    return got.reshape(n * block.shape[0], RANK)


def shift(value, axis, n, by):
    return lax.ppermute(value, axis, [(i, (i + by) % n) for i in range(n)])


def piece(block, i, n):
    rows = block.shape[0] // n
    return lax.dynamic_slice_in_dim(block, (i & (n - 1)) * rows, rows, 0)


def scatter_shift(block, axis, n):
    me = lax.axis_index(axis)
    got = [shift(piece(block, me + by, n), axis, n, by) for by in range(1, n)]
    return sum((g.astype(F32) for g in got), piece(block, me, n).astype(F32)).astype(BF16)


def gather_shift(block, axis, n):
    return [block] + [shift(block, axis, n, by) for by in range(1, n)]


def in_order(blocks, axis):
    n = len(blocks)
    me = lax.axis_index(axis)
    held = jnp.concatenate(blocks)
    return jnp.concatenate([piece(held, me - i + n, n) for i in range(n)])


def add(*values):
    return sum(v.astype(F32) for v in values)


def add_four(v):
    own, one, two, three = (x.astype(F32) for x in v)
    return (own + two) + (one + three)


def trade(value):
    return shift(value, "core", 2, 1)


def all_sum(value, sizes):
    value = value + trade(value)
    value = add_four(gather_shift(value, "x", sizes["x"]))
    for step in (1, 2, 4):
        value = value + lax.ppermute(value, "z", [(i, i ^ step) for i in range(sizes["z"])])
    return value


TN = (((0,), (0,)), ((), ()))
NN = (((1,), (0,)), ((), ()))
NT = (((1,), (1,)), ((), ()))


def dot(a, b, dims):
    return lax.dot_general(a, b, dims, preferred_element_type=F32)


def shards(sizes, whole, momentum, gradient, right_basis):
    nx, nz, ny = sizes["x"], sizes["z"], sizes["row"]
    pos = jnp.stack([lax.axis_index(axis) for axis in ("core", "x", "row")]).astype(jnp.int32)
    core = lax.axis_index("core")
    low = core == 0
    half = momentum.shape[0] // 2
    cut = half * 2 // 3
    basis_half = right_basis.astype(BF16)

    def part_of(which):
        mom = lax.dynamic_slice_in_dim(momentum, which * half, half, 0)
        grad = lax.dynamic_slice_in_dim(gradient, which * half, half, 0)
        return dot((mom.astype(F32) + grad.astype(F32)).astype(BF16), basis_half, NN)

    away = part_of(1 - core).astype(BF16)
    got = jnp.concatenate([trade(away[: half // 2]), trade(away[half // 2 :])])
    part = (part_of(core) + got.astype(F32)).astype(BF16)
    first, second = part[:cut], part[cut:]
    first = scatter_shift(first, "x", nx)
    second = scatter_swap(second, "z", nz)
    second = scatter_shift(second, "x", nx)
    first = scatter_swap(first, "z", nz)
    first = gather_swap(first, "z", nz)
    second = in_order(gather_shift(second, "x", nx), "x")
    first = gather_shift(first, "x", nx)
    second = gather_swap(second, "z", nz)

    held = jnp.concatenate(first)
    gram_part = (dot(held, held, TN) + dot(second, second, TN)).astype(BF16)
    gram = add(piece(gram_part, core, 2), trade(piece(gram_part, 1 - core, 2))).astype(BF16)
    mine = jnp.concatenate([in_order(first, "x"), second])
    other = trade(mine)
    gram = scatter_shift(gram, "row", ny)
    gram = jnp.concatenate(gather_shift(gram, "row", ny))
    blended = (momentum.astype(F32) + gradient.astype(F32)).astype(BF16)
    projected = jnp.concatenate([jnp.where(low, mine, other), jnp.where(low, other, mine)])
    cross = dot(blended, projected, TN).astype(BF16)
    gram, cross = lax.optimization_barrier((gram, cross))
    cross = gather_shift(cross, "row", ny)
    inverse = inverse_factor(pos, gram, trade(gram))
    back_proj = dot(add_four(cross).astype(BF16), inverse, NT)
    col_sq = all_sum(jnp.sum(back_proj * back_proj, axis=0, keepdims=True), sizes)
    ortho_half = dot(projected, inverse, NT).astype(BF16)
    low_rank = dot(ortho_half, back_proj.astype(BF16), NT)
    new_momentum = (blended.astype(F32) - error_share * low_rank).astype(BF16)
    new_basis = back_proj / (jnp.sqrt(col_sq) + epsilon)
    product = dot(ortho_half, new_basis.astype(BF16), NT)
    direction = (product * math.sqrt(whole / RANK)).astype(BF16)
    return (new_momentum, new_basis, direction)


def solution(mesh):
    sizes = {"row": 4, "z": 8, "x": 4, "core": 2}
    inner = Mesh(mesh.devices.reshape(tuple(sizes.values())), tuple(sizes))
    col = ("z", "x", "core")

    def step(momentum, gradient, right_basis):
        whole = momentum.shape[0] * momentum.shape[1]
        body = lambda *args: shards(sizes, whole, *args)
        return jax.shard_map(
            body,
            mesh=inner,
            in_specs=(P("row", col), P("row", col), P(col, None)),
            out_specs=(P("row", col), P(col, None), P("row", col)),
            check_vma=False,
        )(momentum, gradient, right_basis)

    return step
```

```python
import math

import jax
import jax.numpy as jnp
from jax import lax
from jax.experimental import pallas as pl
from jax.experimental.pallas import tpu as pltpu
from jax.sharding import Mesh
from jax.sharding import PartitionSpec as P

RANK = 512
NB = 128
F32 = jnp.float32
BF16 = jnp.bfloat16
error_share = 0.05
epsilon = 1e-06


def split(value):
    high = value.astype(BF16)
    return high, (value - high.astype(F32)).astype(BF16)


def product3(left, right, dims):
    left_high, left_low = split(left)
    right_high, right_low = split(right)
    dot = lambda a, b: lax.dot_general(a, b, dims, preferred_element_type=F32)
    return dot(left_high, right_high) + (dot(left_high, right_low) + dot(left_low, right_high))


def factor_block(w_ref, sub, lane):
    groups = NB // 8
    wide = (8, NB)
    row_of = lambda value, k: jnp.broadcast_to(value[k : k + 1, :], wide)
    columns = lambda value, at: [jnp.broadcast_to(value[:, at + j : at + j + 1], wide) for j in range(8)]
    for b in range(groups):
        r0 = 8 * b
        mine = (lane >= r0) & (lane < r0 + 8)
        more = b + 1 < groups
        top = w_ref[r0 : r0 + 8, :]
        cols = columns(top, r0)
        top = jnp.where(mine, jnp.where(lane - r0 == sub, 1.0, 0.0), top)
        if more:
            below = w_ref[r0 + 8 : r0 + 16, :]
            next_cols = columns(below, r0)
            below = jnp.where(mine, 0.0, below)
        pivots = jnp.ones(wide, F32)
        rows, inverse, coef = [], [], {}
        for k in range(8):
            pivot = row_of(cols[k], k)
            recip = 1.0 / pivot
            pivots = jnp.where(sub == k, pivot, pivots)
            row = row_of(top, k)
            factor = jnp.where(sub > k, cols[k] * recip, 0.0)
            if more:
                next_factor = next_cols[k] * recip
            for j in range(k + 1, 8):
                coef[k, j] = row_of(cols[j], k)
                cols[j] = cols[j] - factor * coef[k, j]
                if more:
                    next_cols[j] = next_cols[j] - next_factor * coef[k, j]
            top = top - factor * row
            if more:
                below = below - next_factor * row
            rows.append(row)
            inverse.append(recip)
        w_ref[r0 : r0 + 8, :] = top * lax.rsqrt(pivots)
        if more:
            w_ref[r0 + 8 : r0 + 16, :] = below
        for v in range(b + 2, groups):
            q = 8 * v
            low = w_ref[q : q + 8, :]
            lead = columns(low, r0)
            low = jnp.where(mine, 0.0, low)
            for k in range(8):
                factor = lead[k] * inverse[k]
                for j in range(k + 1, 8):
                    lead[j] = lead[j] - factor * coef[k, j]
                low = low - factor * rows[k]
            w_ref[q : q + 8, :] = low


def chol_kernel(pos_ref, mine_ref, other_ref, half_ref, o_ref, w_ref):
    sub = lax.broadcasted_iota(jnp.int32, (8, NB), 0)
    lane = lax.broadcasted_iota(jnp.int32, (8, NB), 1)
    lower = lax.broadcasted_iota(jnp.int32, (NB, NB), 0) >= lax.broadcasted_iota(jnp.int32, (NB, NB), 1)
    pieces = 4
    tall = mine_ref.shape[0] // pieces
    for j in range(pieces):
        at = ((pos_ref[2] - j) & (pieces - 1)) * tall
        here = slice(j * tall, (j + 1) * tall)
        o_ref[pl.ds(pl.multiple_of(at + pos_ref[0] * (RANK // 2), tall), tall), :] = mine_ref[here, :].astype(F32)
        o_ref[pl.ds(pl.multiple_of(at + (1 - pos_ref[0]) * (RANK // 2), tall), tall), :] = other_ref[here, :].astype(F32)

    def step(p, carry):
        at = pl.multiple_of(p * NB, NB)
        here = pl.ds(at, NB)
        w_ref[...] = o_ref[here, here]
        factor_block(w_ref, sub, lane)
        block = jnp.where(lower, w_ref[...], 0.0)
        panel = product3(block, o_ref[here, :], (((1,), (0,)), ((), ())))
        o_ref[here, :] = panel
        o_ref[here, here] = block
        for k in range(RANK // NB - 1):

            @pl.when(p == k)
            def _(k=k):
                done = (k + 1) * NB
                o_ref[done:, k * NB : done] = jnp.zeros((RANK - done, NB), F32)
                rows = o_ref[k * NB : done, :]
                o_ref[done:, :] -= product3(panel[:, done:], rows, (((0,), (0,)), ((), ())))

        return carry

    lax.fori_loop(0, RANK // NB, step, 0)
    row = lax.broadcasted_iota(jnp.int32, (RANK, RANK), 0)
    col = lax.broadcasted_iota(jnp.int32, (RANK, RANK), 1)
    half_ref[...] = jnp.where(row >= col, o_ref[...], 0.0).astype(BF16)


SMEM = pl.BlockSpec(memory_space=pltpu.SMEM)
VMEM = pl.BlockSpec(memory_space=pltpu.VMEM)


def local(kernel, name, ins, outs, flops, scratch=()):
    shapes = [jax.ShapeDtypeStruct(shape, dtype) for shape, dtype in outs]
    moved = sum(v.size * v.dtype.itemsize for v in (*ins, *shapes))
    return pl.pallas_call(
        kernel,
        out_shape=shapes,
        in_specs=[SMEM] + [VMEM] * (len(ins) - 1),
        out_specs=[VMEM] * len(outs),
        scratch_shapes=[pltpu.VMEM(shape, dtype) for shape, dtype in scratch],
        compiler_params=pltpu.CompilerParams(vmem_limit_bytes=6 * 1024 * 1024),
        cost_estimate=pl.CostEstimate(flops=flops, bytes_accessed=moved, transcendentals=0),
        name=name,
    )(*ins)


def inverse_factor(pos, mine, other):
    square = (RANK, RANK)
    return local(
        chol_kernel,
        "inverse_factor",
        (pos, mine, other),
        [(square, BF16)],
        20_000_000_000,
        [(square, F32), ((NB, NB), F32)],
    )[0]


def swap(pieces, axis):
    return lax.all_to_all(pieces, axis, 0, 0, tiled=True)


def scatter_swap(block, axis, n):
    got = swap(block.reshape(n, block.shape[0] // n, RANK), axis)
    return jnp.sum(got.astype(F32), axis=0).astype(BF16)


def gather_swap(block, axis, n):
    got = swap(jnp.broadcast_to(block[None], (n, *block.shape)), axis)
    return got.reshape(n * block.shape[0], RANK)


def shift(value, axis, n, by):
    return lax.ppermute(value, axis, [(i, (i + by) % n) for i in range(n)])


def piece(block, i, n):
    rows = block.shape[0] // n
    return lax.dynamic_slice_in_dim(block, (i & (n - 1)) * rows, rows, 0)


def scatter_shift(block, axis, n):
    me = lax.axis_index(axis)
    got = [shift(piece(block, me + by, n), axis, n, by) for by in range(1, n)]
    return sum((g.astype(F32) for g in got), piece(block, me, n).astype(F32)).astype(BF16)


def gather_shift(block, axis, n):
    return [block] + [shift(block, axis, n, by) for by in range(1, n)]


def in_order(blocks, axis):
    n = len(blocks)
    me = lax.axis_index(axis)
    held = jnp.concatenate(blocks)
    return jnp.concatenate([piece(held, me - i + n, n) for i in range(n)])


def add(*values):
    return sum(v.astype(F32) for v in values)


def add_four(v):
    own, one, two, three = (x.astype(F32) for x in v)
    return (own + two) + (one + three)


def trade(value):
    return shift(value, "core", 2, 1)


TN = (((0,), (0,)), ((), ()))
NN = (((1,), (0,)), ((), ()))
NT = (((1,), (1,)), ((), ()))


def dot(a, b, dims):
    return lax.dot_general(a, b, dims, preferred_element_type=F32)


def shards(sizes, whole, momentum, gradient, right_basis):
    nx, nz, ny = sizes["x"], sizes["z"], sizes["row"]
    pos = jnp.stack([lax.axis_index(axis) for axis in ("core", "x", "row")]).astype(jnp.int32)
    core = lax.axis_index("core")
    low = core == 0
    half = momentum.shape[0] // 2
    cut = half * 2 // 3
    basis_half = right_basis.astype(BF16)

    def part_of(which, start, size):
        mom = lax.dynamic_slice_in_dim(momentum, which * half + start, size, 0)
        grad = lax.dynamic_slice_in_dim(gradient, which * half + start, size, 0)
        return dot((mom.astype(F32) + grad.astype(F32)).astype(BF16), basis_half, NN)

    away = part_of(1 - core, 0, half).astype(BF16)
    got = [trade(away[i * half // 3 : (i + 1) * half // 3]) for i in range(3)]
    first = (part_of(core, 0, cut) + jnp.concatenate(got[:2]).astype(F32)).astype(BF16)
    second = (part_of(core, cut, half - cut) + got[2].astype(F32)).astype(BF16)
    first = scatter_shift(first, "x", nx)
    second = scatter_swap(second, "z", nz)
    second = scatter_shift(second, "x", nx)
    first = scatter_swap(first, "z", nz)
    first = gather_swap(first, "z", nz)
    second = in_order(gather_shift(second, "x", nx), "x")
    first = gather_shift(first, "x", nx)
    second = gather_swap(second, "z", nz)

    held = jnp.concatenate(first)
    gram_part = (dot(held, held, TN) + dot(second, second, TN)).astype(BF16)
    gram = add(piece(gram_part, core, 2), trade(piece(gram_part, 1 - core, 2))).astype(BF16)
    mine = jnp.concatenate([in_order(first, "x"), second])
    other = trade(mine)
    gram, other = lax.optimization_barrier((scatter_shift(gram, "row", ny), other))
    gram = jnp.concatenate(gather_shift(gram, "row", ny))
    blended = (momentum.astype(F32) + gradient.astype(F32)).astype(BF16)
    projected = jnp.concatenate([jnp.where(low, mine, other), jnp.where(low, other, mine)])
    cross = dot(blended, projected, TN).astype(BF16)
    gram, cross = lax.optimization_barrier((gram, cross))
    cross = gather_shift(cross, "row", ny)
    inverse = inverse_factor(pos, gram, trade(gram))
    back_proj = dot(add_four(cross).astype(BF16), inverse, NT)
    ortho_half = dot(projected, inverse, NT).astype(BF16)
    low_rank = dot(ortho_half, back_proj.astype(BF16), NT)
    new_momentum = (blended.astype(F32) - error_share * low_rank).astype(BF16)
    col_sq = jnp.sum(back_proj * back_proj, axis=0, keepdims=True)
    got, ortho_half = lax.optimization_barrier((trade(col_sq), ortho_half))
    got, new_momentum = lax.optimization_barrier((gather_shift(col_sq + got, "x", nx), new_momentum))
    col_sq = add_four(got)
    col_sq = col_sq + lax.ppermute(col_sq, "z", [(i, i ^ 1) for i in range(nz)])
    col_sq = add_four([col_sq] + [shift(col_sq, "z", nz, by) for by in (2, 4, 6)])
    new_basis = back_proj / (jnp.sqrt(col_sq) + epsilon)
    product = dot(ortho_half, new_basis.astype(BF16), NT)
    direction = (product * math.sqrt(whole / RANK)).astype(BF16)
    return (new_momentum, new_basis, direction)


def solution(mesh):
    sizes = {"row": 4, "z": 8, "x": 4, "core": 2}
    inner = Mesh(mesh.devices.reshape(tuple(sizes.values())), tuple(sizes))
    col = ("z", "x", "core")

    def step(momentum, gradient, right_basis):
        whole = momentum.shape[0] * momentum.shape[1]
        body = lambda *args: shards(sizes, whole, *args)
        return jax.shard_map(
            body,
            mesh=inner,
            in_specs=(P("row", col), P("row", col), P(col, None)),
            out_specs=(P("row", col), P(col, None), P("row", col)),
            check_vma=False,
        )(momentum, gradient, right_basis)

    return step
```

```python
import math

import jax
import jax.numpy as jnp
from jax import lax
from jax.experimental import pallas as pl
from jax.experimental.pallas import tpu as pltpu
from jax.sharding import Mesh
from jax.sharding import PartitionSpec as P

RANK = 512
NB = 128
F32 = jnp.float32
BF16 = jnp.bfloat16
error_share = 0.05
epsilon = 1e-06


def split(value):
    high = value.astype(BF16)
    return high, (value - high.astype(F32)).astype(BF16)


def product3(left, right, dims):
    left_high, left_low = split(left)
    right_high, right_low = split(right)
    dot = lambda a, b: lax.dot_general(a, b, dims, preferred_element_type=F32)
    return dot(left_high, right_high) + (dot(left_high, right_low) + dot(left_low, right_high))


def factor_block(w_ref, sub, lane):
    groups = NB // 8
    wide = (8, NB)
    row_of = lambda value, k: jnp.broadcast_to(value[k : k + 1, :], wide)
    columns = lambda value, at: [jnp.broadcast_to(value[:, at + j : at + j + 1], wide) for j in range(8)]
    for b in range(groups):
        r0 = 8 * b
        mine = (lane >= r0) & (lane < r0 + 8)
        more = b + 1 < groups
        top = w_ref[r0 : r0 + 8, :]
        cols = columns(top, r0)
        top = jnp.where(mine, jnp.where(lane - r0 == sub, 1.0, 0.0), top)
        if more:
            below = w_ref[r0 + 8 : r0 + 16, :]
            next_cols = columns(below, r0)
            below = jnp.where(mine, 0.0, below)
        pivots = jnp.ones(wide, F32)
        rows, inverse, coef = [], [], {}
        for k in range(8):
            pivot = row_of(cols[k], k)
            recip = 1.0 / pivot
            pivots = jnp.where(sub == k, pivot, pivots)
            row = row_of(top, k)
            factor = jnp.where(sub > k, cols[k] * recip, 0.0)
            if more:
                next_factor = next_cols[k] * recip
            for j in range(k + 1, 8):
                coef[k, j] = row_of(cols[j], k)
                cols[j] = cols[j] - factor * coef[k, j]
                if more:
                    next_cols[j] = next_cols[j] - next_factor * coef[k, j]
            top = top - factor * row
            if more:
                below = below - next_factor * row
            rows.append(row)
            inverse.append(recip)
        w_ref[r0 : r0 + 8, :] = top * lax.rsqrt(pivots)
        if more:
            w_ref[r0 + 8 : r0 + 16, :] = below
        for v in range(b + 2, groups):
            q = 8 * v
            low = w_ref[q : q + 8, :]
            lead = columns(low, r0)
            low = jnp.where(mine, 0.0, low)
            for k in range(8):
                factor = lead[k] * inverse[k]
                for j in range(k + 1, 8):
                    lead[j] = lead[j] - factor * coef[k, j]
                low = low - factor * rows[k]
            w_ref[q : q + 8, :] = low


def eliminate(o_ref, w_ref, first, last):
    sub = lax.broadcasted_iota(jnp.int32, (8, NB), 0)
    lane = lax.broadcasted_iota(jnp.int32, (8, NB), 1)
    lower = lax.broadcasted_iota(jnp.int32, (NB, NB), 0) >= lax.broadcasted_iota(jnp.int32, (NB, NB), 1)

    def step(p, carry):
        here = pl.ds(pl.multiple_of(p * NB, NB), NB)
        w_ref[...] = o_ref[here, here]
        factor_block(w_ref, sub, lane)
        block = jnp.where(lower, w_ref[...], 0.0)
        panel = product3(block, o_ref[here, :], (((1,), (0,)), ((), ())))
        o_ref[here, :] = panel
        o_ref[here, here] = block
        for k in range(first, min(last, RANK // NB - 1)):

            @pl.when(p == k)
            def _(k=k):
                done = (k + 1) * NB
                o_ref[done:, k * NB : done] = jnp.zeros((RANK - done, NB), F32)
                rows = o_ref[k * NB : done, :]
                o_ref[done:, :] -= product3(panel[:, done:], rows, (((0,), (0,)), ((), ())))

        return carry

    lax.fori_loop(first, last, step, 0)


def first_kernel(pos_ref, mine_ref, other_ref, o_ref, w_ref):
    pieces = 4
    tall = mine_ref.shape[0] // pieces
    for j in range(pieces):
        at = ((pos_ref[2] - j) & (pieces - 1)) * tall
        here = slice(j * tall, (j + 1) * tall)
        o_ref[pl.ds(pl.multiple_of(at + pos_ref[0] * (RANK // 2), tall), tall), :] = mine_ref[here, :].astype(F32)
        o_ref[pl.ds(pl.multiple_of(at + (1 - pos_ref[0]) * (RANK // 2), tall), tall), :] = other_ref[here, :].astype(F32)
    eliminate(o_ref, w_ref, 0, RANK // NB // 2)


def second_kernel(pos_ref, g_ref, half_ref, o_ref, w_ref):
    o_ref[...] = g_ref[...]
    eliminate(o_ref, w_ref, RANK // NB // 2, RANK // NB)
    row = lax.broadcasted_iota(jnp.int32, (RANK, RANK), 0)
    col = lax.broadcasted_iota(jnp.int32, (RANK, RANK), 1)
    half_ref[...] = jnp.where(row >= col, o_ref[...], 0.0).astype(BF16)


SMEM = pl.BlockSpec(memory_space=pltpu.SMEM)
VMEM = pl.BlockSpec(memory_space=pltpu.VMEM)


def local(kernel, name, ins, outs, flops, scratch=()):
    shapes = [jax.ShapeDtypeStruct(shape, dtype) for shape, dtype in outs]
    moved = sum(v.size * v.dtype.itemsize for v in (*ins, *shapes))
    return pl.pallas_call(
        kernel,
        out_shape=shapes,
        in_specs=[SMEM] + [VMEM] * (len(ins) - 1),
        out_specs=[VMEM] * len(outs),
        scratch_shapes=[pltpu.VMEM(shape, dtype) for shape, dtype in scratch],
        compiler_params=pltpu.CompilerParams(vmem_limit_bytes=6 * 1024 * 1024),
        cost_estimate=pl.CostEstimate(flops=flops, bytes_accessed=moved, transcendentals=0),
        name=name,
    )(*ins)


SQUARE = (RANK, RANK)
FLOPS = 10_000_000_000


def first_half(pos, mine, other):
    return local(first_kernel, "first_half", (pos, mine, other), [(SQUARE, F32)], FLOPS, [((NB, NB), F32)])[0]


def second_half(pos, state):
    scratch = [(SQUARE, F32), ((NB, NB), F32)]
    return local(second_kernel, "second_half", (pos, state), [(SQUARE, BF16)], FLOPS, scratch)[0]


def swap(pieces, axis):
    return lax.all_to_all(pieces, axis, 0, 0, tiled=True)


def scatter_swap(block, axis, n):
    got = swap(block.reshape(n, block.shape[0] // n, RANK), axis)
    return jnp.sum(got.astype(F32), axis=0).astype(BF16)


def gather_swap(block, axis, n):
    got = swap(jnp.broadcast_to(block[None], (n, *block.shape)), axis)
    return got.reshape(n * block.shape[0], RANK)


def shift(value, axis, n, by):
    return lax.ppermute(value, axis, [(i, (i + by) % n) for i in range(n)])


def piece(block, i, n):
    rows = block.shape[0] // n
    return lax.dynamic_slice_in_dim(block, (i & (n - 1)) * rows, rows, 0)


def scatter_shift(block, axis, n):
    me = lax.axis_index(axis)
    got = [shift(piece(block, me + by, n), axis, n, by) for by in range(1, n)]
    return sum((g.astype(F32) for g in got), piece(block, me, n).astype(F32)).astype(BF16)


def gather_shift(block, axis, n):
    return [block] + [shift(block, axis, n, by) for by in range(1, n)]


def in_order(blocks, axis):
    n = len(blocks)
    me = lax.axis_index(axis)
    held = jnp.concatenate(blocks)
    return jnp.concatenate([piece(held, me - i + n, n) for i in range(n)])


def add(*values):
    return sum(v.astype(F32) for v in values)


def add_four(v):
    own, one, two, three = (x.astype(F32) for x in v)
    return (own + two) + (one + three)


def trade(value):
    return shift(value, "core", 2, 1)


TN = (((0,), (0,)), ((), ()))
NN = (((1,), (0,)), ((), ()))
NT = (((1,), (1,)), ((), ()))


def dot(a, b, dims):
    return lax.dot_general(a, b, dims, preferred_element_type=F32)


def shards(sizes, whole, momentum, gradient, right_basis):
    nx, nz, ny = sizes["x"], sizes["z"], sizes["row"]
    pos = jnp.stack([lax.axis_index(axis) for axis in ("core", "x", "row")]).astype(jnp.int32)
    core = lax.axis_index("core")
    low = core == 0
    half = momentum.shape[0] // 2
    cut = half * 2 // 3
    basis_half = right_basis.astype(BF16)

    def part_of(which, start, size):
        mom = lax.dynamic_slice_in_dim(momentum, which * half + start, size, 0)
        grad = lax.dynamic_slice_in_dim(gradient, which * half + start, size, 0)
        return dot((mom.astype(F32) + grad.astype(F32)).astype(BF16), basis_half, NN)

    away = part_of(1 - core, 0, half).astype(BF16)
    got = [trade(away[i * half // 3 : (i + 1) * half // 3]) for i in range(3)]
    first = (part_of(core, 0, cut) + jnp.concatenate(got[:2]).astype(F32)).astype(BF16)
    second = (part_of(core, cut, half - cut) + got[2].astype(F32)).astype(BF16)
    first = scatter_shift(first, "x", nx)
    second = scatter_swap(second, "z", nz)
    second = scatter_shift(second, "x", nx)
    first = scatter_swap(first, "z", nz)
    first = gather_swap(first, "z", nz)
    second = in_order(gather_shift(second, "x", nx), "x")
    first = gather_shift(first, "x", nx)
    second = gather_swap(second, "z", nz)

    held = jnp.concatenate(first)
    gram_part = (dot(held, held, TN) + dot(second, second, TN)).astype(BF16)
    gram = add(piece(gram_part, core, 2), trade(piece(gram_part, 1 - core, 2))).astype(BF16)
    mine = jnp.concatenate([in_order(first, "x"), second])
    other = trade(mine)
    gram, other = lax.optimization_barrier((scatter_shift(gram, "row", ny), other))
    gram = jnp.concatenate(gather_shift(gram, "row", ny))
    blended = (momentum.astype(F32) + gradient.astype(F32)).astype(BF16)
    projected = jnp.concatenate([jnp.where(low, mine, other), jnp.where(low, other, mine)])
    cross = dot(blended, projected, TN).astype(BF16)
    gram, cross = lax.optimization_barrier((gram, cross))
    early = [shift(cross, "row", ny, by) for by in (1, 2)]
    state = first_half(pos, gram, trade(gram))
    late, state = lax.optimization_barrier((cross, state))
    cross = [cross, *early, shift(late, "row", ny, 3)]
    inverse = second_half(pos, state)
    back_proj = dot(add_four(cross).astype(BF16), inverse, NT)
    ortho_half = dot(projected, inverse, NT).astype(BF16)
    low_rank = dot(ortho_half, back_proj.astype(BF16), NT)
    new_momentum = (blended.astype(F32) - error_share * low_rank).astype(BF16)
    col_sq = jnp.sum(back_proj * back_proj, axis=0, keepdims=True)
    got, ortho_half = lax.optimization_barrier((trade(col_sq), ortho_half))
    got, new_momentum = lax.optimization_barrier((gather_shift(col_sq + got, "x", nx), new_momentum))
    col_sq = add_four(got)
    col_sq = col_sq + lax.ppermute(col_sq, "z", [(i, i ^ 1) for i in range(nz)])
    col_sq = add_four([col_sq] + [shift(col_sq, "z", nz, by) for by in (2, 4, 6)])
    new_basis = back_proj / (jnp.sqrt(col_sq) + epsilon)
    product = dot(ortho_half, new_basis.astype(BF16), NT)
    direction = (product * math.sqrt(whole / RANK)).astype(BF16)
    return (new_momentum, new_basis, direction)


def solution(mesh):
    sizes = {"row": 4, "z": 8, "x": 4, "core": 2}
    inner = Mesh(mesh.devices.reshape(tuple(sizes.values())), tuple(sizes))
    col = ("z", "x", "core")

    def step(momentum, gradient, right_basis):
        whole = momentum.shape[0] * momentum.shape[1]
        body = lambda *args: shards(sizes, whole, *args)
        return jax.shard_map(
            body,
            mesh=inner,
            in_specs=(P("row", col), P("row", col), P(col, None)),
            out_specs=(P("row", col), P(col, None), P("row", col)),
            check_vma=False,
        )(momentum, gradient, right_basis)

    return step
```

```python
import math

import jax
import jax.numpy as jnp
from jax import lax
from jax.experimental import pallas as pl
from jax.experimental.pallas import tpu as pltpu
from jax.sharding import Mesh
from jax.sharding import PartitionSpec as P

RANK = 512
NB = 128
F32 = jnp.float32
BF16 = jnp.bfloat16
error_share = 0.05
epsilon = 1e-06


def split(value):
    high = value.astype(BF16)
    return high, (value - high.astype(F32)).astype(BF16)


def product3(left, right, dims):
    left_high, left_low = split(left)
    right_high, right_low = split(right)
    dot = lambda a, b: lax.dot_general(a, b, dims, preferred_element_type=F32)
    return dot(left_high, right_high) + (dot(left_high, right_low) + dot(left_low, right_high))


def factor_block(w_ref, sub, lane):
    groups = NB // 8
    wide = (8, NB)
    row_of = lambda value, k: jnp.broadcast_to(value[k : k + 1, :], wide)
    columns = lambda value, at: [jnp.broadcast_to(value[:, at + j : at + j + 1], wide) for j in range(8)]
    for b in range(groups):
        r0 = 8 * b
        mine = (lane >= r0) & (lane < r0 + 8)
        more = b + 1 < groups
        top = w_ref[r0 : r0 + 8, :]
        cols = columns(top, r0)
        top = jnp.where(mine, jnp.where(lane - r0 == sub, 1.0, 0.0), top)
        if more:
            below = w_ref[r0 + 8 : r0 + 16, :]
            next_cols = columns(below, r0)
            below = jnp.where(mine, 0.0, below)
        pivots = jnp.ones(wide, F32)
        rows, inverse, coef = [], [], {}
        for k in range(8):
            pivot = row_of(cols[k], k)
            recip = 1.0 / pivot
            pivots = jnp.where(sub == k, pivot, pivots)
            row = row_of(top, k)
            factor = jnp.where(sub > k, cols[k] * recip, 0.0)
            if more:
                next_factor = next_cols[k] * recip
            for j in range(k + 1, 8):
                coef[k, j] = row_of(cols[j], k)
                cols[j] = cols[j] - factor * coef[k, j]
                if more:
                    next_cols[j] = next_cols[j] - next_factor * coef[k, j]
            top = top - factor * row
            if more:
                below = below - next_factor * row
            rows.append(row)
            inverse.append(recip)
        w_ref[r0 : r0 + 8, :] = top * lax.rsqrt(pivots)
        if more:
            w_ref[r0 + 8 : r0 + 16, :] = below
        for v in range(b + 2, groups):
            q = 8 * v
            low = w_ref[q : q + 8, :]
            lead = columns(low, r0)
            low = jnp.where(mine, 0.0, low)
            for k in range(8):
                factor = lead[k] * inverse[k]
                for j in range(k + 1, 8):
                    lead[j] = lead[j] - factor * coef[k, j]
                low = low - factor * rows[k]
            w_ref[q : q + 8, :] = low


def eliminate(o_ref, w_ref, first, last):
    sub = lax.broadcasted_iota(jnp.int32, (8, NB), 0)
    lane = lax.broadcasted_iota(jnp.int32, (8, NB), 1)
    lower = lax.broadcasted_iota(jnp.int32, (NB, NB), 0) >= lax.broadcasted_iota(jnp.int32, (NB, NB), 1)

    def step(p, carry):
        here = pl.ds(pl.multiple_of(p * NB, NB), NB)
        w_ref[...] = o_ref[here, here]
        factor_block(w_ref, sub, lane)
        block = jnp.where(lower, w_ref[...], 0.0)
        panel = product3(block, o_ref[here, :], (((1,), (0,)), ((), ())))
        o_ref[here, :] = panel
        o_ref[here, here] = block
        for k in range(first, min(last, RANK // NB - 1)):

            @pl.when(p == k)
            def _(k=k):
                done = (k + 1) * NB
                o_ref[done:, k * NB : done] = jnp.zeros((RANK - done, NB), F32)
                rows = o_ref[k * NB : done, :]
                o_ref[done:, :] -= product3(panel[:, done:], rows, (((0,), (0,)), ((), ())))

        return carry

    lax.fori_loop(first, last, step, 0)


def first_kernel(pos_ref, mine_ref, other_ref, o_ref, w_ref):
    pieces = 4
    tall = mine_ref.shape[0] // pieces
    for j in range(pieces):
        at = ((pos_ref[2] - j) & (pieces - 1)) * tall
        here = slice(j * tall, (j + 1) * tall)
        o_ref[pl.ds(pl.multiple_of(at + pos_ref[0] * (RANK // 2), tall), tall), :] = mine_ref[here, :].astype(F32)
        o_ref[pl.ds(pl.multiple_of(at + (1 - pos_ref[0]) * (RANK // 2), tall), tall), :] = other_ref[here, :].astype(F32)
    eliminate(o_ref, w_ref, 0, RANK // NB // 2)


def second_kernel(pos_ref, g_ref, half_ref, o_ref, w_ref):
    o_ref[...] = g_ref[...]
    eliminate(o_ref, w_ref, RANK // NB // 2, RANK // NB)
    row = lax.broadcasted_iota(jnp.int32, (RANK, RANK), 0)
    col = lax.broadcasted_iota(jnp.int32, (RANK, RANK), 1)
    half_ref[...] = jnp.where(row >= col, o_ref[...], 0.0).astype(BF16)


SMEM = pl.BlockSpec(memory_space=pltpu.SMEM)
VMEM = pl.BlockSpec(memory_space=pltpu.VMEM)


def local(kernel, name, ins, outs, flops, scratch=()):
    shapes = [jax.ShapeDtypeStruct(shape, dtype) for shape, dtype in outs]
    moved = sum(v.size * v.dtype.itemsize for v in (*ins, *shapes))
    return pl.pallas_call(
        kernel,
        out_shape=shapes,
        in_specs=[SMEM] + [VMEM] * (len(ins) - 1),
        out_specs=[VMEM] * len(outs),
        scratch_shapes=[pltpu.VMEM(shape, dtype) for shape, dtype in scratch],
        compiler_params=pltpu.CompilerParams(vmem_limit_bytes=6 * 1024 * 1024),
        cost_estimate=pl.CostEstimate(flops=flops, bytes_accessed=moved, transcendentals=0),
        name=name,
    )(*ins)


SQUARE = (RANK, RANK)
FLOPS = 10_000_000_000


def first_half(pos, mine, other):
    return local(first_kernel, "first_half", (pos, mine, other), [(SQUARE, F32)], FLOPS, [((NB, NB), F32)])[0]


def second_half(pos, state):
    scratch = [(SQUARE, F32), ((NB, NB), F32)]
    return local(second_kernel, "second_half", (pos, state), [(SQUARE, BF16)], FLOPS, scratch)[0]


def swap(pieces, axis):
    return lax.all_to_all(pieces, axis, 0, 0, tiled=True)


def scatter_swap(block, axis, n):
    got = swap(block.reshape(n, block.shape[0] // n, RANK), axis)
    return jnp.sum(got.astype(F32), axis=0).astype(BF16)


def gather_swap(block, axis, n):
    got = swap(jnp.broadcast_to(block[None], (n, *block.shape)), axis)
    return got.reshape(n * block.shape[0], RANK)


def shift(value, axis, n, by):
    return lax.ppermute(value, axis, [(i, (i + by) % n) for i in range(n)])


def piece(block, i, n):
    rows = block.shape[0] // n
    return lax.dynamic_slice_in_dim(block, (i & (n - 1)) * rows, rows, 0)


def scatter_shift(block, axis, n):
    me = lax.axis_index(axis)
    got = [shift(piece(block, me + by, n), axis, n, by) for by in range(1, n)]
    return sum((g.astype(F32) for g in got), piece(block, me, n).astype(F32)).astype(BF16)


def gather_shift(block, axis, n):
    return [block] + [shift(block, axis, n, by) for by in range(1, n)]


def in_order(blocks, axis):
    n = len(blocks)
    me = lax.axis_index(axis)
    held = jnp.concatenate(blocks)
    return jnp.concatenate([piece(held, me - i + n, n) for i in range(n)])


def add(*values):
    return sum(v.astype(F32) for v in values)


def add_four(v):
    own, one, two, three = (x.astype(F32) for x in v)
    return (own + two) + (one + three)


def trade(value):
    return shift(value, "core", 2, 1)


def all_sum(value, sizes):
    value = value + trade(value)
    value = add_four(gather_shift(value, "x", sizes["x"]))
    for step in (1, 2, 4):
        value = value + lax.ppermute(value, "z", [(i, i ^ step) for i in range(sizes["z"])])
    return value


TN = (((0,), (0,)), ((), ()))
NN = (((1,), (0,)), ((), ()))
NT = (((1,), (1,)), ((), ()))


def dot(a, b, dims):
    return lax.dot_general(a, b, dims, preferred_element_type=F32)


def shards(sizes, whole, momentum, gradient, right_basis):
    nx, nz, ny = sizes["x"], sizes["z"], sizes["row"]
    pos = jnp.stack([lax.axis_index(axis) for axis in ("core", "x", "row")]).astype(jnp.int32)
    core = lax.axis_index("core")
    low = core == 0
    half = momentum.shape[0] // 2
    cut = half * 2 // 3
    basis_half = right_basis.astype(BF16)

    def part_of(which):
        mom = lax.dynamic_slice_in_dim(momentum, which * half, half, 0)
        grad = lax.dynamic_slice_in_dim(gradient, which * half, half, 0)
        return dot((mom.astype(F32) + grad.astype(F32)).astype(BF16), basis_half, NN)

    away = part_of(1 - core).astype(BF16)
    got = jnp.concatenate([trade(away[: half // 2]), trade(away[half // 2 :])])
    part = (part_of(core) + got.astype(F32)).astype(BF16)
    first, second = part[:cut], part[cut:]
    first = scatter_shift(first, "x", nx)
    second = scatter_swap(second, "z", nz)
    second = scatter_shift(second, "x", nx)
    first = scatter_swap(first, "z", nz)
    first = gather_swap(first, "z", nz)
    second = in_order(gather_shift(second, "x", nx), "x")
    first = gather_shift(first, "x", nx)
    second = gather_swap(second, "z", nz)

    held = jnp.concatenate(first)
    gram_part = (dot(held, held, TN) + dot(second, second, TN)).astype(BF16)
    gram = add(piece(gram_part, core, 2), trade(piece(gram_part, 1 - core, 2))).astype(BF16)
    mine = jnp.concatenate([in_order(first, "x"), second])
    other = trade(mine)
    gram, other = lax.optimization_barrier((scatter_shift(gram, "row", ny), other))
    gram = jnp.concatenate(gather_shift(gram, "row", ny))
    blended = (momentum.astype(F32) + gradient.astype(F32)).astype(BF16)
    projected = jnp.concatenate([jnp.where(low, mine, other), jnp.where(low, other, mine)])
    cross = dot(blended, projected, TN).astype(BF16)
    gram, cross = lax.optimization_barrier((gram, cross))
    early = [shift(cross, "row", ny, by) for by in (1, 2)]
    state = first_half(pos, gram, trade(gram))
    late, state = lax.optimization_barrier((cross, state))
    cross = [cross, *early, shift(late, "row", ny, 3)]
    inverse = second_half(pos, state)
    back_proj = dot(add_four(cross).astype(BF16), inverse, NT)
    col_sq = all_sum(jnp.sum(back_proj * back_proj, axis=0, keepdims=True), sizes)
    ortho_half = dot(projected, inverse, NT).astype(BF16)
    low_rank = dot(ortho_half, back_proj.astype(BF16), NT)
    new_momentum = (blended.astype(F32) - error_share * low_rank).astype(BF16)
    new_basis = back_proj / (jnp.sqrt(col_sq) + epsilon)
    product = dot(ortho_half, new_basis.astype(BF16), NT)
    direction = (product * math.sqrt(whole / RANK)).astype(BF16)
    return (new_momentum, new_basis, direction)


def solution(mesh):
    sizes = {"row": 4, "z": 8, "x": 4, "core": 2}
    inner = Mesh(mesh.devices.reshape(tuple(sizes.values())), tuple(sizes))
    col = ("z", "x", "core")

    def step(momentum, gradient, right_basis):
        whole = momentum.shape[0] * momentum.shape[1]
        body = lambda *args: shards(sizes, whole, *args)
        return jax.shard_map(
            body,
            mesh=inner,
            in_specs=(P("row", col), P("row", col), P(col, None)),
            out_specs=(P("row", col), P(col, None), P("row", col)),
            check_vma=False,
        )(momentum, gradient, right_basis)

    return step
```

```python
import math

import jax
import jax.numpy as jnp
from jax import lax
from jax.experimental import pallas as pl
from jax.experimental.pallas import tpu as pltpu
from jax.sharding import Mesh
from jax.sharding import PartitionSpec as P

RANK = 512
NB = 128
F32 = jnp.float32
BF16 = jnp.bfloat16
error_share = 0.05
epsilon = 1e-06


def split(value):
    high = value.astype(BF16)
    return high, (value - high.astype(F32)).astype(BF16)


def product3(left, right, dims):
    left_high, left_low = split(left)
    right_high, right_low = split(right)
    dot = lambda a, b: lax.dot_general(a, b, dims, preferred_element_type=F32)
    return dot(left_high, right_high) + (dot(left_high, right_low) + dot(left_low, right_high))


def factor_block(w_ref, sub, lane):
    groups = NB // 8
    wide = (8, NB)
    row_of = lambda value, k: jnp.broadcast_to(value[k : k + 1, :], wide)
    columns = lambda value, at: [jnp.broadcast_to(value[:, at + j : at + j + 1], wide) for j in range(8)]
    for b in range(groups):
        r0 = 8 * b
        mine = (lane >= r0) & (lane < r0 + 8)
        more = b + 1 < groups
        top = w_ref[r0 : r0 + 8, :]
        cols = columns(top, r0)
        top = jnp.where(mine, jnp.where(lane - r0 == sub, 1.0, 0.0), top)
        if more:
            below = w_ref[r0 + 8 : r0 + 16, :]
            next_cols = columns(below, r0)
            below = jnp.where(mine, 0.0, below)
        pivots = jnp.ones(wide, F32)
        rows, inverse, coef = [], [], {}
        for k in range(8):
            pivot = row_of(cols[k], k)
            recip = 1.0 / pivot
            pivots = jnp.where(sub == k, pivot, pivots)
            row = row_of(top, k)
            factor = jnp.where(sub > k, cols[k] * recip, 0.0)
            if more:
                next_factor = next_cols[k] * recip
            for j in range(k + 1, 8):
                coef[k, j] = row_of(cols[j], k)
                cols[j] = cols[j] - factor * coef[k, j]
                if more:
                    next_cols[j] = next_cols[j] - next_factor * coef[k, j]
            top = top - factor * row
            if more:
                below = below - next_factor * row
            rows.append(row)
            inverse.append(recip)
        w_ref[r0 : r0 + 8, :] = top * lax.rsqrt(pivots)
        if more:
            w_ref[r0 + 8 : r0 + 16, :] = below
        for v in range(b + 2, groups):
            q = 8 * v
            low = w_ref[q : q + 8, :]
            lead = columns(low, r0)
            low = jnp.where(mine, 0.0, low)
            for k in range(8):
                factor = lead[k] * inverse[k]
                for j in range(k + 1, 8):
                    lead[j] = lead[j] - factor * coef[k, j]
                low = low - factor * rows[k]
            w_ref[q : q + 8, :] = low


def chol_kernel(pos_ref, mine_ref, other_ref, half_ref, o_ref, w_ref):
    sub = lax.broadcasted_iota(jnp.int32, (8, NB), 0)
    lane = lax.broadcasted_iota(jnp.int32, (8, NB), 1)
    lower = lax.broadcasted_iota(jnp.int32, (NB, NB), 0) >= lax.broadcasted_iota(jnp.int32, (NB, NB), 1)
    wide_lane = lax.broadcasted_iota(jnp.int32, (NB, RANK), 1)
    tall_row = lax.broadcasted_iota(jnp.int32, (RANK, NB), 0)
    pieces = 4
    tall = mine_ref.shape[0] // pieces
    for j in range(pieces):
        at = ((pos_ref[2] - j) & (pieces - 1)) * tall
        here = slice(j * tall, (j + 1) * tall)
        o_ref[pl.ds(pl.multiple_of(at + pos_ref[0] * (RANK // 2), tall), tall), :] = mine_ref[here, :].astype(F32)
        o_ref[pl.ds(pl.multiple_of(at + (1 - pos_ref[0]) * (RANK // 2), tall), tall), :] = other_ref[here, :].astype(F32)

    def step(p, carry):
        at = pl.multiple_of(p * NB, NB)
        here = pl.ds(at, NB)
        w_ref[...] = o_ref[here, here]
        factor_block(w_ref, sub, lane)
        block = jnp.where(lower, w_ref[...], 0.0)
        panel = product3(block, o_ref[here, :], (((1,), (0,)), ((), ())))
        o_ref[here, :] = panel
        o_ref[here, here] = block
        rest = jnp.where(wide_lane >= at + NB, panel, 0.0)
        o_ref[:, here] = jnp.where(tall_row >= at + NB, 0.0, o_ref[:, here])
        o_ref[...] -= product3(rest, o_ref[here, :], (((0,), (0,)), ((), ())))
        return carry

    lax.fori_loop(0, RANK // NB, step, 0)
    row = lax.broadcasted_iota(jnp.int32, (RANK, RANK), 0)
    col = lax.broadcasted_iota(jnp.int32, (RANK, RANK), 1)
    half_ref[...] = jnp.where(row >= col, o_ref[...], 0.0).astype(BF16)


SMEM = pl.BlockSpec(memory_space=pltpu.SMEM)
VMEM = pl.BlockSpec(memory_space=pltpu.VMEM)


def local(kernel, name, ins, outs, flops, scratch=()):
    shapes = [jax.ShapeDtypeStruct(shape, dtype) for shape, dtype in outs]
    moved = sum(v.size * v.dtype.itemsize for v in (*ins, *shapes))
    return pl.pallas_call(
        kernel,
        out_shape=shapes,
        in_specs=[SMEM] + [VMEM] * (len(ins) - 1),
        out_specs=[VMEM] * len(outs),
        scratch_shapes=[pltpu.VMEM(shape, dtype) for shape, dtype in scratch],
        compiler_params=pltpu.CompilerParams(vmem_limit_bytes=6 * 1024 * 1024),
        cost_estimate=pl.CostEstimate(flops=flops, bytes_accessed=moved, transcendentals=0),
        name=name,
    )(*ins)


def inverse_factor(pos, mine, other):
    square = (RANK, RANK)
    return local(
        chol_kernel,
        "inverse_factor",
        (pos, mine, other),
        [(square, BF16)],
        20_000_000_000,
        [(square, F32), ((NB, NB), F32)],
    )[0]


def swap(pieces, axis):
    return lax.all_to_all(pieces, axis, 0, 0, tiled=True)


def scatter_swap(block, axis, n):
    got = swap(block.reshape(n, block.shape[0] // n, RANK), axis)
    return jnp.sum(got.astype(F32), axis=0).astype(BF16)


def gather_swap(block, axis, n):
    got = swap(jnp.broadcast_to(block[None], (n, *block.shape)), axis)
    return got.reshape(n * block.shape[0], RANK)


def shift(value, axis, n, by):
    return lax.ppermute(value, axis, [(i, (i + by) % n) for i in range(n)])


def piece(block, i, n):
    rows = block.shape[0] // n
    return lax.dynamic_slice_in_dim(block, (i & (n - 1)) * rows, rows, 0)


def scatter_shift(block, axis, n):
    me = lax.axis_index(axis)
    got = [shift(piece(block, me + by, n), axis, n, by) for by in range(1, n)]
    return sum((g.astype(F32) for g in got), piece(block, me, n).astype(F32)).astype(BF16)


def gather_shift(block, axis, n):
    return [block] + [shift(block, axis, n, by) for by in range(1, n)]


def in_order(blocks, axis):
    n = len(blocks)
    me = lax.axis_index(axis)
    held = jnp.concatenate(blocks)
    return jnp.concatenate([piece(held, me - i + n, n) for i in range(n)])


def add(*values):
    return sum(v.astype(F32) for v in values)


def add_four(v):
    own, one, two, three = (x.astype(F32) for x in v)
    return (own + two) + (one + three)


def trade(value):
    return shift(value, "core", 2, 1)


TN = (((0,), (0,)), ((), ()))
NN = (((1,), (0,)), ((), ()))
NT = (((1,), (1,)), ((), ()))


def dot(a, b, dims):
    return lax.dot_general(a, b, dims, preferred_element_type=F32)


def shards(sizes, whole, momentum, gradient, right_basis):
    nx, nz, ny = sizes["x"], sizes["z"], sizes["row"]
    pos = jnp.stack([lax.axis_index(axis) for axis in ("core", "x", "row")]).astype(jnp.int32)
    core = lax.axis_index("core")
    low = core == 0
    half = momentum.shape[0] // 2
    cut = half * 2 // 3
    basis_half = right_basis.astype(BF16)

    def part_of(which):
        mom = lax.dynamic_slice_in_dim(momentum, which * half, half, 0)
        grad = lax.dynamic_slice_in_dim(gradient, which * half, half, 0)
        return dot((mom.astype(F32) + grad.astype(F32)).astype(BF16), basis_half, NN)

    away = part_of(1 - core).astype(BF16)
    got = jnp.concatenate([trade(away[: half // 2]), trade(away[half // 2 :])])
    part = (part_of(core) + got.astype(F32)).astype(BF16)
    first, second = part[:cut], part[cut:]
    first = scatter_shift(first, "x", nx)
    second = scatter_swap(second, "z", nz)
    second = scatter_shift(second, "x", nx)
    first = scatter_swap(first, "z", nz)
    first = gather_swap(first, "z", nz)
    second = in_order(gather_shift(second, "x", nx), "x")
    first = gather_shift(first, "x", nx)
    second = gather_swap(second, "z", nz)

    held = jnp.concatenate(first)
    gram_part = (dot(held, held, TN) + dot(second, second, TN)).astype(BF16)
    gram = add(piece(gram_part, core, 2), trade(piece(gram_part, 1 - core, 2))).astype(BF16)
    mine = jnp.concatenate([in_order(first, "x"), second])
    other = trade(mine)
    gram, other = lax.optimization_barrier((scatter_shift(gram, "row", ny), other))
    gram = jnp.concatenate(gather_shift(gram, "row", ny))
    blended = (momentum.astype(F32) + gradient.astype(F32)).astype(BF16)
    projected = jnp.concatenate([jnp.where(low, mine, other), jnp.where(low, other, mine)])
    cross = dot(blended, projected, TN).astype(BF16)
    gram, cross = lax.optimization_barrier((gram, cross))
    cross = gather_shift(cross, "row", ny)
    inverse = inverse_factor(pos, gram, trade(gram))
    back_proj = dot(add_four(cross).astype(BF16), inverse, NT)
    ortho_half = dot(projected, inverse, NT).astype(BF16)
    low_rank = dot(ortho_half, back_proj.astype(BF16), NT)
    new_momentum = (blended.astype(F32) - error_share * low_rank).astype(BF16)
    col_sq = jnp.sum(back_proj * back_proj, axis=0, keepdims=True)
    got, ortho_half = lax.optimization_barrier((trade(col_sq), ortho_half))
    got, new_momentum = lax.optimization_barrier((gather_shift(col_sq + got, "x", nx), new_momentum))
    col_sq = add_four(got)
    col_sq = col_sq + lax.ppermute(col_sq, "z", [(i, i ^ 1) for i in range(nz)])
    col_sq = add_four([col_sq] + [shift(col_sq, "z", nz, by) for by in (2, 4, 6)])
    new_basis = back_proj / (jnp.sqrt(col_sq) + epsilon)
    product = dot(ortho_half, new_basis.astype(BF16), NT)
    direction = (product * math.sqrt(whole / RANK)).astype(BF16)
    return (new_momentum, new_basis, direction)


def solution(mesh):
    sizes = {"row": 4, "z": 8, "x": 4, "core": 2}
    inner = Mesh(mesh.devices.reshape(tuple(sizes.values())), tuple(sizes))
    col = ("z", "x", "core")

    def step(momentum, gradient, right_basis):
        whole = momentum.shape[0] * momentum.shape[1]
        body = lambda *args: shards(sizes, whole, *args)
        return jax.shard_map(
            body,
            mesh=inner,
            in_specs=(P("row", col), P("row", col), P(col, None)),
            out_specs=(P("row", col), P(col, None), P("row", col)),
            check_vma=False,
        )(momentum, gradient, right_basis)

    return step
```
